32 devices in a mesh: lon: 8 (over y, x, core), lat: 4 (over z).
Axes of the slice: x: 2, y: 2, z: 4, core: 2. Of those that a mesh axis runs over, the one named last changes fastest.
Arguments:
- eta_init: float32 [2, 512, 8192], P(None, 'lat', 'lon'), may hold values from -6 to 6
- depth: float32 [512, 8192], P('lat', 'lon'), may hold values from 0.1 to 1
- sea_mask: int32 [512, 8192], P('lat', 'lon'), may hold values 0 or 1
- probe_cells: int32 [32, 2, 192], P(('lon', 'lat')), may hold values from 0 to 8191, as said below
- elapsed_record: bfloat16 [32, 2, 192, 1024], P(('lon', 'lat')), may hold values from -6 to 6
- gauge_kernels: bfloat16 [32, 32, 192, 1024], P(('lon', 'lat')), may hold values from -0.013671875 to 0.013671875
Outputs:
- eta_final: float32 [2, 512, 8192], P(None, 'lat', 'lon')
- shore_outlook: float32 [32, 2, 8, 32], P(('lon', 'lat'))
The draws below stay inside these ranges and needn't reach their ends.
Inputs may be any that keep to these rules, and one draw needn't show every extreme that they name: probe_cells[g, 0, k] is a row below 512 and probe_cells[g, 1, k] a column below 8192. All probes of segment g lie in latitude band b = g % 4, rows 128 * b to 128 * b + 127. Of one segment's 192 probes at most 32 lie in one longitude sector of 1024 columns, and every segment has exactly 32 in some sector.
All inputs are finite; a program needn't handle non-finite values. No bound on the sum of `sea_mask` on one device may be relied on, other than what follows from the above.
Results may differ from the reference program's by a relative error of at most 0.0003.
Values sent between devices are 32-bit elements; how exact they have to be, the bound alone decides.
No kernel may reach another device: no remote copies, remote signals or barrier semaphores. Data moves between devices by JAX's collectives and lax.ppermute only.
A program may use at most 192 MiB of HBM per device.

```python
import math
import jax
import jax.numpy as jnp
from jax import lax

CLAT = 128
CLON = 1024
MEMBERS = 2
STEPS = 8
PROBES = 192
CAP = 32
COAST_SEG = 32
LAGS = 1024
NLAT = 512
NLON = 8192
SEGS = 32
N_LON = 8
N_LAT = 4


def draw_probe_cells(key, part):
    seg_count = N_LON * N_LAT
    sector_count = PROBES // CAP
    key_list = jax.random.split(jax.random.fold_in(key, 17), 5)
    hot_sector = jax.random.randint(key_list[0], (), 0, N_LON)
    sector_scores = jax.random.randint(key_list[1], (seg_count, N_LON), 0, 1 << 20)
    sector_scores = jnp.where(jnp.arange(N_LON)[None, :] == hot_sector, -1, sector_scores)
    chosen = jnp.argsort(sector_scores, axis=1, stable=True)[:, :sector_count]
    sectors = jnp.repeat(chosen, CAP, axis=1)
    mixing = jnp.argsort(jax.random.randint(key_list[2], (seg_count, PROBES), 0, 1 << 20), axis=1, stable=True)
    sectors = jnp.take_along_axis(sectors, mixing, axis=1)
    band_ids = (jnp.arange(seg_count) % N_LAT)[:, None]
    local_rows = jax.random.randint(key_list[3], (seg_count, PROBES), 0, CLAT)
    local_cols = jax.random.randint(key_list[4], (seg_count, PROBES), 0, CLON)
    rows_out = band_ids * CLAT + local_rows
    cols_out = sectors * CLON + local_cols
    return jnp.stack([rows_out, cols_out], axis=1).astype(jnp.int32)


def with_ends(drawn, rng, least, top_value):
    spot = [jax.random.randint(jax.random.fold_in(rng, axis), (), 0, length) for axis, length in enumerate(drawn.shape)]
    widest = drawn.shape.index(max(drawn.shape))
    next_to = spot[:widest] + [(spot[widest] + 1) % drawn.shape[widest]] + spot[widest + 1:]
    return drawn.at[tuple(spot)].set(least).at[tuple(next_to)].set(top_value)


def block_levels(key, extent, cuts, smallest, high):
    loudness = 1.0
    for axis_at, blocks in cuts:
        steps = jax.random.uniform(jax.random.fold_in(jax.random.fold_in(key, 6), axis_at), (blocks,), jnp.float32, smallest / len(cuts), high / len(cuts))
        loudness = loudness * jnp.repeat(jnp.exp(steps), extent[axis_at] // blocks).reshape((-1,) + (1,) * (len(extent) - 1 - axis_at))
    return loudness


def gaussian(stream_key, shape, scale, bound, cuts=(), kind=jnp.bfloat16):
    factor_of = block_levels(stream_key, shape, cuts, -0.22, 0.18) if cuts else 1.0
    drawn = jax.random.normal(stream_key, shape, jnp.float32) * scale * factor_of
    return jnp.minimum(jnp.maximum(drawn, -bound), bound).astype(kind)


def setup_inputs(seed: int = 0) -> dict:
    keys = jax.random.split(jax.random.key(seed), 7)
    eta_init = gaussian(keys[0], (MEMBERS, NLAT, NLON), 1.0, 6.0, ((1, 4), (2, 8)), jnp.float32)
    depth = jnp.clip(jnp.exp(math.log(1.0) - 2.3025851 * jax.random.uniform(keys[1], (NLAT, NLON), jnp.float32) ** block_levels(keys[1], (NLAT, NLON), ((0, 4), (1, 8)), -0.2, 0.2)), 0.1, 1.0)
    sea_mask = with_ends((jax.random.randint(keys[2], (NLAT, NLON), 0, 10) < 9).astype(jnp.int32), jax.random.fold_in(keys[2], 1), 0, 1)
    probe_cells = draw_probe_cells(jax.random.fold_in(keys[6], 71), 0)
    elapsed_record = gaussian(keys[4], (SEGS, MEMBERS, PROBES, LAGS), 1.0, 6.0, ((0, 32),))
    gauge_kernels = gaussian(keys[5], (SEGS, COAST_SEG, PROBES, LAGS), (PROBES * LAGS) ** -0.5, 0.013671875, ((0, 32),))
    return dict(eta_init=eta_init, depth=depth, sea_mask=sea_mask, probe_cells=probe_cells, elapsed_record=elapsed_record, gauge_kernels=gauge_kernels)


def courant_for(total_lat, spacing):
    coldest = math.cos(0.5 * total_lat * spacing)
    return 0.95 * coldest / math.sqrt(1.0 + coldest * coldest)

def advance(elevation_field, east_flow, north_flow, wet_depth, latitude, spacing, courant):
    centre = jnp.cos(latitude)[:, None]
    north_side = jnp.cos(latitude + 0.5 * spacing)[:, None]
    east_new = east_flow[..., :, :-1] - courant / centre * (elevation_field[..., :, 1:] - elevation_field[..., :, :-1])
    north_new = north_flow[..., :-1, :] - courant * (elevation_field[..., 1:, :] - elevation_field[..., :-1, :])
    east_flux = jnp.sqrt(wet_depth[:, 1:] * wet_depth[:, :-1]) * east_new
    north_flux = jnp.sqrt(wet_depth[1:, :] * wet_depth[:-1, :]) * north_side[:-1] * north_new
    change = east_flux[..., 1:-1, 1:] - east_flux[..., 1:-1, :-1] + (north_flux[..., 1:, 1:-1] - north_flux[..., :-1, 1:-1])
    surface_new = elevation_field[..., 1:-1, 1:-1] - courant / centre[1:-1] * change
    return (surface_new, east_new[..., 1:-1, 1:], north_new[..., 1:, 1:-1])

def wrap_pad(values):
    beside_all = jnp.concatenate([values[..., -1:], values, values[..., :1]], axis=-1)
    widths = [(0, 0)] * (values.ndim - 2) + [(1, 1), (0, 0)]
    return jnp.pad(beside_all, widths)

def interval_estimate(segment_parts):
    kernel_factors, past_samples, recent_interval = segment_parts
    lag_count = kernel_factors.shape[2]
    step_count = recent_interval.shape[0]
    series = jnp.concatenate([jnp.transpose(recent_interval[::-1], (1, 2, 0)), past_samples.astype(jnp.float32)], axis=2)
    windows = jnp.stack([series[:, :, step_count - ahead_step:step_count - ahead_step + lag_count] for ahead_step in range(1, step_count + 1)], axis=1)
    return jnp.einsum('cpl,mtpl->mtc', kernel_factors.astype(jnp.float32), windows, precision=lax.Precision.HIGHEST)

def reference(eta_init, depth, sea_mask, probe_cells, elapsed_record, gauge_kernels):
    total_lat = eta_init.shape[1]
    total_lon = eta_init.shape[2]
    spacing = 2.0 * math.pi / total_lon
    courant = courant_for(total_lat, spacing)
    sea_float = sea_mask.astype(jnp.float32)
    wet_wide = wrap_pad(depth * sea_float)
    row_ids = jnp.arange(-1, total_lat + 1, dtype=jnp.int32).astype(jnp.float32)
    latitude = -0.5 * total_lat * spacing + (row_ids + 0.5) * spacing
    elevation_field = eta_init * sea_float
    east_flow = jnp.zeros_like(elevation_field)
    north_flow = jnp.zeros_like(elevation_field)
    flat_index = probe_cells[:, 0, :] * total_lon + probe_cells[:, 1, :]
    recorded = []
    for step_index in range(STEPS):
        elevation_field, east_flow, north_flow = advance(wrap_pad(elevation_field), wrap_pad(east_flow), wrap_pad(north_flow), wet_wide, latitude, spacing, courant)
        recorded.append(elevation_field.reshape(elevation_field.shape[0], -1)[:, flat_index])
    gauge_measures = jnp.transpose(jnp.stack(recorded), (2, 0, 1, 3))
    shore_outlook = lax.map(interval_estimate, (gauge_kernels, elapsed_record, gauge_measures))
    return (elevation_field, shore_outlook)
```

```python
import functools
import math

import jax
import jax.numpy as jnp
from jax import lax
from jax.experimental import pallas as pl
from jax.experimental.pallas import tpu as pltpu
from jax.sharding import PartitionSpec as P

STEPS = 8
CAP = 32
LANES = 128
SUB = 8
HALO = 8
KTILE = 16
VMEM_LIMIT = 48 * 1024 * 1024


def courant_for(total_lat, spacing):
    coldest = math.cos(0.5 * total_lat * spacing)
    return 0.95 * coldest / math.sqrt(1.0 + coldest * coldest)


def nt(a, b, precision=None):
    return lax.dot_general(
        a, b, (((1,), (1,)), ((), ())), preferred_element_type=jnp.float32, precision=precision
    )


def iota(shape, axis):
    return lax.broadcasted_iota(jnp.int32, shape, axis)


def table_kernel(lat_cells, lon_cells, lat_count, lon_count, pitch, cells_ref, out_ref, pick_ref):
    probes = cells_ref.shape[1]
    rows = cells_ref[0:1, :]
    cols = cells_ref[1:2, :]
    for band in range(lat_count - 1, 0, -1):
        rows = rows - jnp.where(rows >= band * lat_cells, lat_cells, 0)
    sector = jnp.zeros_like(cols)
    for s in range(1, lon_count):
        sector = sector + jnp.where(cols >= s * lon_cells, 1, 0)
    cols = cols - sector * lon_cells
    tiles = lon_cells // LANES
    tile = jnp.zeros_like(cols)
    for t in range(1, tiles):
        tile = tile + jnp.where(cols >= t * LANES, 1, 0)
    lane = cols - tile * LANES
    low = cols < HALO
    high = cols >= lon_cells - HALO
    tile = jnp.where(low | high, tiles, tile)
    lane = jnp.where(low, LANES - 2 * HALO + cols, lane)
    lane = jnp.where(high, cols - (lon_cells - 2 * HALO), lane)
    place = (tile * (2 * (STEPS + 1)) + 1) * pitch + HALO + rows
    code = place * LANES + lane
    hits = (iota((lon_count, probes), 0) == sector).astype(jnp.float32)
    before = (iota((probes, probes), 0) < iota((probes, probes), 1)).astype(jnp.bfloat16)
    counts = lax.dot_general(
        hits.astype(jnp.bfloat16), before, (((1,), (0,)), ((), ())), preferred_element_type=jnp.float32
    )
    rank = jnp.sum(hits * counts, axis=0, keepdims=True)
    slots = lon_count * CAP
    key = sector * CAP + rank.astype(jnp.int32)
    pick = (iota((slots, probes), 0) == key).astype(jnp.float32).astype(jnp.bfloat16)
    pick_ref[...] = pick
    digit_row = iota((SUB, probes), 0)
    digits = jnp.where(digit_row == 0, code & 255, 0)
    digits = jnp.where(digit_row == 1, (code >> 8) & 255, digits)
    digits = jnp.where(digit_row == 2, code >> 16, digits)
    sent = nt(digits.astype(jnp.float32).astype(jnp.bfloat16), pick)
    sent = sent[0:1] + 256.0 * sent[1:2] + 65536.0 * sent[2:3]
    sent = sent.astype(jnp.int32)
    out_ref[...] = jnp.zeros_like(out_ref)
    for s in range(lon_count):
        out_ref[s, :, 0:CAP] = sent[:, s * CAP : (s + 1) * CAP]


def recent_kernel(g_ref, pick_ref, out_ref, lags_ref):
    coast = g_ref.shape[0]
    probes = g_ref.shape[1]
    first = (iota((SUB, LANES), 0) == iota((SUB, LANES), 1)).astype(jnp.float32).astype(jnp.bfloat16)
    for c in range(coast):
        lags_ref[c * SUB : (c + 1) * SUB, :] = nt(first, g_ref[c])
    size = coast * SUB
    r = iota((size, size), 0)
    q = iota((size, size), 1)
    order = ((r & (coast - 1)) == (q >> 3)) & ((r // coast) == (q & 7))
    order = order.astype(jnp.float32).astype(jnp.bfloat16)
    lags = lax.dot_general(
        order,
        lags_ref[...].astype(jnp.bfloat16),
        (((1,), (0,)), ((), ())),
        preferred_element_type=jnp.float32,
    )
    out_ref[...] = nt(lags.astype(jnp.bfloat16), pick_ref[...]).astype(jnp.bfloat16)


def past_kernel(members, g_ref, e_ref, out_ref, acc_ref):
    coast, ktile, lag_count = g_ref.shape
    step = pl.program_id(0)
    past = e_ref[...].reshape(members * ktile, lag_count).astype(jnp.float32)
    lane = iota(past.shape, 1)
    shifted = []
    for t in range(1, STEPS + 1):
        moved = jnp.where(lane >= t, pltpu.roll(past, t, axis=1), 0.0)
        shifted.append(moved.astype(jnp.bfloat16))
    windows = jnp.concatenate(shifted, axis=0)
    part = nt(g_ref[...].reshape(coast * ktile, lag_count), windows)

    @pl.when(step == 0)
    def _():
        acc_ref[...] = part

    @pl.when(step > 0)
    def _():
        acc_ref[...] += part

    @pl.when(step == pl.num_programs(0) - 1)
    def _():
        shape = acc_ref.shape
        same = (iota(shape, 0) & (ktile - 1)) == (iota(shape, 1) & (ktile - 1))
        kept = jnp.where(same, acc_ref[...], 0.0)
        kept = jnp.sum(kept.reshape(coast, ktile, shape[1]), axis=1)
        wins = members * STEPS
        w = iota((wins, shape[1]), 0)
        col = iota((wins, shape[1]), 1)
        m = w >> 3
        t = w & 7
        fold = ((col // ktile) == t * members + m).astype(jnp.float32)
        out_ref[...] = nt(fold, kept, precision=lax.Precision.HIGHEST)


def rim_kernel(members, side_ref, eta0, eta1, dep0, dep1, sea0, sea1, top_ref, bot_ref, a_ref, b_ref):
    rows = eta0.shape[1]
    odd = side_ref[0] == 1
    width = top_ref.shape[2]
    lane8 = iota((SUB, LANES), 1)

    def emit(row, west, east):
        one = jnp.zeros_like(west[0])
        two = jnp.zeros_like(west[0])
        for i in range(members + 1):
            here = (lane8 >= i * HALO) & (lane8 < (i + 1) * HALO)
            w = west[i] if i == 0 else pltpu.roll(west[i], i * HALO, axis=1)
            one = jnp.where(here, w, one)
            e = pltpu.roll(east[i], (i + 1) * HALO, axis=1)
            two = jnp.where(here, e, two)
        a_ref[row : row + SUB, :] = jnp.where(odd, one, two)
        b_ref[row : row + SUB, :] = jnp.where(odd, two, one)

    for halo_ref, row in ((top_ref, 0), (bot_ref, rows + HALO)):
        emit(
            row,
            [halo_ref[i, :, 0:LANES] for i in range(members + 1)],
            [halo_ref[i, :, width - LANES : width] for i in range(members + 1)],
        )
    for blk in range(rows // SUB):
        at = slice(blk * SUB, (blk + 1) * SUB)
        s0 = sea0[at, :].astype(jnp.float32)
        s1 = sea1[at, :].astype(jnp.float32)
        emit(
            HALO + blk * SUB,
            [eta0[i, at, :] * s0 for i in range(members)] + [dep0[at, :] * s0],
            [eta1[i, at, :] * s1 for i in range(members)] + [dep1[at, :] * s1],
        )


def wave_kernel(
    members, pitch, idx_ref, side_ref, eta_ref, dep_ref, sea_ref, top_ref, bot_ref, a_ref, b_ref, fac_ref,
    out_ref, smp_ref, hist, wet, east, north, flux, ce, cn,
):
    rows = eta_ref.shape[1]
    lon_cells = eta_ref.shape[2]
    tiles = lon_cells // LANES
    total = rows + 2 * HALO
    blocks = total // SUB
    lane = iota((SUB, LANES), 1)
    odd = side_ref[0] == 1
    zero = jnp.zeros((SUB, LANES), jnp.float32)

    def at(t, m, q):
        return ((t * members + m) * (STEPS + 1) + q) * pitch

    def fill(row, values):
        for t in range(tiles):
            for m in range(members):
                hist[pl.ds(at(t, m, 0) + row, SUB), :] = values[m][t]
            wet[pl.ds(t * pitch + row, SUB), :] = values[members][t]
        a = a_ref[pl.ds(row, SUB), :]
        b = b_ref[pl.ds(row, SUB), :]
        left = jnp.where(odd, a, b)
        right = jnp.where(odd, b, a)
        for i in range(members + 1):
            own_right = pltpu.roll(values[i][tiles - 1], 2 * HALO, axis=1)
            own_left = pltpu.roll(values[i][0], LANES - 2 * HALO, axis=1)
            far_right = pltpu.roll(right, (2 * HALO - i * HALO) % LANES, axis=1)
            far_left = pltpu.roll(left, (LANES - 3 * HALO - i * HALO) % LANES, axis=1)
            v = jnp.where(lane < 2 * HALO, own_right, far_right)
            v = jnp.where(lane < 3 * HALO, v, 0.0)
            v = jnp.where(lane >= LANES - 3 * HALO, far_left, v)
            v = jnp.where(lane >= LANES - 2 * HALO, own_left, v)
            if i < members:
                hist[pl.ds(at(tiles, i, 0) + row, SUB), :] = v
            else:
                wet[pl.ds(tiles * pitch + row, SUB), :] = v

    for ref, row in ((top_ref, 0), (bot_ref, rows + HALO)):
        fill(row, [[ref[i, :, t * LANES : (t + 1) * LANES] for t in range(tiles)] for i in range(members + 1)])

    def fill_block(blk, carry):
        row = pl.multiple_of(blk * SUB, SUB)
        sea = [sea_ref[pl.ds(row, SUB), t * LANES : (t + 1) * LANES].astype(jnp.float32) for t in range(tiles)]
        values = [
            [eta_ref[m, pl.ds(row, SUB), t * LANES : (t + 1) * LANES] * sea[t] for t in range(tiles)]
            for m in range(members)
        ]
        values.append([dep_ref[pl.ds(row, SUB), t * LANES : (t + 1) * LANES] * sea[t] for t in range(tiles)])
        fill(pl.multiple_of(row + HALO, SUB), values)
        return carry

    lax.fori_loop(0, rows // SUB, fill_block, 0)

    for t in range(tiles + 1):
        wet[t * pitch + total : t * pitch + total + SUB, :] = zero
        for m in range(members):
            for q in range(STEPS):
                hist[at(t, m, q) + total : at(t, m, q) + total + SUB, :] = zero
            flux[(t * members + m) * pitch : (t * members + m) * pitch + SUB, :] = zero

    def coefficients(blk, carry):
        row = pl.multiple_of(blk * SUB, SUB)
        fe = fac_ref[0, pl.ds(row, SUB), :]
        fn = fac_ref[1, pl.ds(row, SUB), :]
        w = [wet[pl.ds(t * pitch + row, SUB), :] for t in range(tiles + 1)]
        rolled = [pltpu.roll(v, LANES - 1, axis=1) for v in w]
        for t in range(tiles + 1):
            beside = rolled[t]
            if t < tiles - 1:
                beside = jnp.where(lane == LANES - 1, rolled[t + 1], beside)
            below = wet[pl.ds(t * pitch + row + 1, SUB), :]
            ce[pl.ds(t * pitch + row, SUB), :] = fe * jnp.sqrt(w[t] * beside)
            cn[pl.ds(t * pitch + row, SUB), :] = fn * jnp.sqrt(w[t] * below)
            for m in range(members):
                east[pl.ds((t * members + m) * pitch + row, SUB), :] = zero
                north[pl.ds((t * members + m) * pitch + row, SUB), :] = zero
        return carry

    lax.fori_loop(0, blocks, coefficients, 0)

    def one_step(q, carry):
        def one_block(blk, inner):
            row = pl.multiple_of(blk * SUB, SUB)
            scale = fac_ref[2, pl.ds(row, SUB), :]
            for m in range(members):
                s = [hist[pl.ds(at(t, m, q) + row, SUB), :] for t in range(tiles + 1)]
                rs = [pltpu.roll(v, LANES - 1, axis=1) for v in s]
                rf_before = None
                for t in range(tiles + 1):
                    own = (t * members + m) * pitch + row
                    beside = rs[t]
                    if t < tiles - 1:
                        beside = jnp.where(lane == LANES - 1, rs[t + 1], beside)
                    e = east[pl.ds(own, SUB), :] + (beside - s[t])
                    east[pl.ds(own, SUB), :] = e
                    fe = ce[pl.ds(t * pitch + row, SUB), :] * e
                    rf = pltpu.roll(fe, 1, axis=1)
                    west = rf
                    if 0 < t < tiles:
                        west = jnp.where(lane == 0, rf_before, rf)
                    rf_before = rf
                    below = hist[pl.ds(at(t, m, q) + row + 1, SUB), :]
                    n = north[pl.ds(own, SUB), :] + (below - s[t])
                    north[pl.ds(own, SUB), :] = n
                    fn = cn[pl.ds(t * pitch + row, SUB), :] * n
                    flux[pl.ds(own + SUB, SUB), :] = fn
                    above = flux[pl.ds(own + SUB - 1, SUB), :]
                    hist[pl.ds(at(t, m, q + 1) + row, SUB), :] = s[t] + ((fe - west) + scale * (fn - above))
            return inner

        return lax.fori_loop(0, blocks, one_block, carry)

    lax.fori_loop(0, STEPS, one_step, 0)

    lon_count = smp_ref.shape[0]

    def sample(s, carry):
        acc = zero
        for j in range(CAP):
            code = idx_ref[s, 0, j]
            spot = lax.bitwise_and(code, LANES - 1)
            place = lax.shift_right_logical(code, 7)
            for m in range(members):
                v = hist[pl.ds(place + m * (STEPS + 1) * pitch, SUB, stride=pitch), :]
                target = m * CAP + j
                v = pltpu.roll(v, lax.bitwise_and(target - spot, LANES - 1), axis=1)
                acc = jnp.where(lane == target, v, acc)
        smp_ref[s] = acc
        return carry

    lax.fori_loop(0, lon_count, sample, 0)

    def finish(blk, carry):
        row = pl.multiple_of(blk * SUB, SUB)
        for m in range(members):
            v = [hist[pl.ds(at(t, m, STEPS) + HALO + row, SUB), :] for t in range(tiles + 1)]
            left = pltpu.roll(v[tiles], 2 * HALO, axis=1)
            right = pltpu.roll(v[tiles], LANES - 2 * HALO, axis=1)
            v[0] = jnp.where(lane < HALO, left, v[0])
            v[tiles - 1] = jnp.where(lane >= LANES - HALO, right, v[tiles - 1])
            for t in range(tiles):
                out_ref[m, pl.ds(row, SUB), t * LANES : (t + 1) * LANES] = v[t]
        return carry

    lax.fori_loop(0, rows // SUB, finish, 0)


def shore_kernel(members, rec_ref, gp_ref, prior_ref, out_ref):
    lon_count = rec_ref.shape[0]
    coast = out_ref.shape[1]
    per = LANES // CAP
    lane = iota((SUB, LANES), 1)
    series = []
    for m in range(members):
        row = []
        for tile in range(lon_count // per):
            acc = jnp.zeros((SUB, LANES), jnp.float32)
            for j in range(per):
                v = pltpu.roll(rec_ref[tile * per + j], ((j - m) * CAP) % LANES, axis=1)
                acc = jnp.where((lane >= j * CAP) & (lane < (j + 1) * CAP), v, acc)
            row.append(acc)
        series.append(jnp.concatenate(row, axis=1))
    x = jnp.concatenate(series, axis=0)
    hi = x.astype(jnp.bfloat16)
    rest = x - hi.astype(jnp.float32)
    mid = rest.astype(jnp.bfloat16)
    lo = (rest - mid.astype(jnp.float32)).astype(jnp.bfloat16)
    r = nt(jnp.concatenate([hi, mid, lo], axis=0), gp_ref[...])
    n = members * STEPS
    r = r[0:n] + r[n : 2 * n] + r[2 * n : 3 * n]
    row8 = iota((SUB, LANES), 0)
    per = LANES // coast
    for m in range(members):
        total = jnp.zeros((SUB, LANES), jnp.float32)
        for l in range(STEPS):
            v = r[m * SUB : (m + 1) * SUB, (l // per) * LANES : (l // per + 1) * LANES]
            if l % per:
                v = pltpu.roll(v, LANES - (l % per) * coast, axis=1)
            if l:
                v = jnp.where(row8 >= l, pltpu.roll(v, l, axis=0), 0.0)
            total = total + v
        out_ref[m * SUB : (m + 1) * SUB, :] = prior_ref[m * SUB : (m + 1) * SUB, :] + total[:, 0:coast]


def local(eta_init, depth, sea_mask, probe_cells, elapsed_record, gauge_kernels):
    members, lat_cells, lon_cells = eta_init.shape
    lat_count = lax.axis_size("lat")
    lon_count = lax.axis_size("lon")
    coast, probes, lag_count = gauge_kernels.shape[1:]
    total_lat = lat_cells * lat_count
    total_lon = lon_cells * lon_count
    spacing = 2.0 * math.pi / total_lon
    courant = courant_for(total_lat, spacing)
    tiles = lon_cells // LANES
    total = lat_cells + 2 * HALO
    pitch = total + SUB
    f32 = jnp.float32
    vmem = pl.BlockSpec(memory_space=pltpu.VMEM)
    smem = pl.BlockSpec(memory_space=pltpu.SMEM)
    params = pltpu.CompilerParams(vmem_limit_bytes=VMEM_LIMIT)

    def edge_rows(sl):
        sea = sea_mask[sl].astype(f32)
        return jnp.concatenate([eta_init[:, sl] * sea, (depth[sl] * sea)[None]], axis=0)

    up = [(i, i + 1) for i in range(lat_count - 1)]
    down = [(i + 1, i) for i in range(lat_count - 1)]
    top = lax.ppermute(edge_rows(slice(lat_cells - HALO, lat_cells)), "lat", up)
    bottom = lax.ppermute(edge_rows(slice(0, HALO)), "lat", down)

    sent, pick = pl.pallas_call(
        functools.partial(table_kernel, lat_cells, lon_cells, lat_count, lon_count, pitch),
        out_shape=[
            jax.ShapeDtypeStruct((lon_count, 1, LANES), jnp.int32),
            jax.ShapeDtypeStruct((lon_count * CAP, probes), jnp.bfloat16),
        ],
        in_specs=[vmem],
        out_specs=[vmem, vmem],
        compiler_params=params,
        name="table",
    )(probe_cells[0])
    incoming = lax.all_to_all(sent, "lon", split_axis=0, concat_axis=0, tiled=True)

    prior = pl.pallas_call(
        functools.partial(past_kernel, members),
        grid=(probes // KTILE,),
        out_shape=jax.ShapeDtypeStruct((members * STEPS, coast), f32),
        in_specs=[
            pl.BlockSpec((None, coast, KTILE, lag_count), lambda k: (0, 0, k, 0)),
            pl.BlockSpec((None, members, KTILE, lag_count), lambda k: (0, 0, k, 0)),
        ],
        out_specs=pl.BlockSpec((members * STEPS, coast), lambda k: (0, 0)),
        scratch_shapes=[pltpu.VMEM((coast * KTILE, members * STEPS * KTILE), f32)],
        compiler_params=params,
        cost_estimate=pl.CostEstimate(
            flops=2 * probes * lag_count * coast * members * STEPS * KTILE,
            bytes_accessed=2 * gauge_kernels.size,
            transcendentals=0,
        ),
        name="past",
    )(gauge_kernels, elapsed_record)

    recent = pl.pallas_call(
        recent_kernel,
        grid=(1,),
        out_shape=jax.ShapeDtypeStruct((STEPS * coast, lon_count * CAP), jnp.bfloat16),
        in_specs=[
            pl.BlockSpec((None, coast, probes, LANES), lambda k: (0, 0, 0, 0)),
            pl.BlockSpec((lon_count * CAP, probes), lambda k: (0, 0)),
        ],
        out_specs=pl.BlockSpec((STEPS * coast, lon_count * CAP), lambda k: (0, 0)),
        scratch_shapes=[pltpu.VMEM((STEPS * coast, probes), f32)],
        compiler_params=params,
        name="recent",
    )(gauge_kernels, pick)

    side = lax.rem(lax.axis_index("lon"), 2).astype(jnp.int32)[None]
    first = lambda k: (0, 0, 0)
    last = lambda k: (0, 0, tiles - 1)
    eta_spec = [pl.BlockSpec((members, lat_cells, LANES), f) for f in (first, last)]
    cell_spec = [
        pl.BlockSpec((lat_cells, LANES), f) for f in (lambda k: (0, 0), lambda k: (0, tiles - 1))
    ]
    halo_spec = pl.BlockSpec((members + 1, HALO, lon_cells), first)
    rim_out = pl.BlockSpec((total, LANES), lambda k: (0, 0))
    send_a, send_b = pl.pallas_call(
        functools.partial(rim_kernel, members),
        grid=(1,),
        out_shape=[jax.ShapeDtypeStruct((total, LANES), f32)] * 2,
        in_specs=[smem] + eta_spec + cell_spec + cell_spec + [halo_spec, halo_spec],
        out_specs=[rim_out, rim_out],
        compiler_params=params,
        name="rim",
    )(side, eta_init, eta_init, depth, depth, sea_mask, sea_mask, top, bottom)
    swap_a = [(i, i ^ 1) for i in range(lon_count)]
    swap_b = [((i + 1) % lon_count, ((i ^ 1) + 1) % lon_count) for i in range(lon_count)]
    rim_a = lax.ppermute(send_a, "lon", swap_a)
    rim_b = lax.ppermute(send_b, "lon", swap_b)

    first_row = lax.axis_index("lat") * lat_cells - HALO
    ids = (first_row + jnp.arange(total, dtype=jnp.int32)).astype(f32)
    latitude = -0.5 * total_lat * spacing + (ids + 0.5) * spacing
    scale = courant / jnp.cos(latitude)
    factors = jnp.stack([scale * scale, courant * jnp.cos(latitude + 0.5 * spacing), scale])
    factors = jnp.broadcast_to(factors[:, :, None], (3, total, LANES))

    states = tiles + 1
    eta_final, samples = pl.pallas_call(
        functools.partial(wave_kernel, members, pitch),
        out_shape=[
            jax.ShapeDtypeStruct(eta_init.shape, f32),
            jax.ShapeDtypeStruct((lon_count, SUB, LANES), f32),
        ],
        in_specs=[smem, smem] + [vmem] * 8,
        out_specs=[vmem, vmem],
        scratch_shapes=[
            pltpu.VMEM((states * members * (STEPS + 1) * pitch, LANES), f32),
            pltpu.VMEM((states * pitch, LANES), f32),
            pltpu.VMEM((states * members * pitch, LANES), f32),
            pltpu.VMEM((states * members * pitch, LANES), f32),
            pltpu.VMEM((states * members * pitch, LANES), f32),
            pltpu.VMEM((states * pitch, LANES), f32),
            pltpu.VMEM((states * pitch, LANES), f32),
        ],
        compiler_params=params,
        name="wave",
    )(incoming, side, eta_init, depth, sea_mask, top, bottom, rim_a, rim_b, factors)

    answered = lax.all_to_all(samples, "lon", split_axis=0, concat_axis=0, tiled=True)
    shore = pl.pallas_call(
        functools.partial(shore_kernel, members),
        out_shape=jax.ShapeDtypeStruct((members * STEPS, coast), f32),
        in_specs=[vmem, vmem, vmem],
        out_specs=vmem,
        compiler_params=params,
        name="shore",
    )(answered, recent, prior)
    return eta_final, shore.reshape(1, members, STEPS, coast)


def solution(mesh):
    in_specs = (
        P(None, "lat", "lon"),
        P("lat", "lon"),
        P("lat", "lon"),
        P(("lon", "lat"), None, None),
        P(("lon", "lat"), None, None, None),
        P(("lon", "lat"), None, None, None),
    )
    out_specs = (P(None, "lat", "lon"), P(("lon", "lat"), None, None, None))
    return jax.shard_map(local, mesh=mesh, in_specs=in_specs, out_specs=out_specs, check_vma=False)
```

```python
import functools
import math

import jax
import jax.numpy as jnp
from jax import lax
from jax.experimental import pallas as pl
from jax.experimental.pallas import tpu as pltpu
from jax.sharding import PartitionSpec as P

STEPS = 8
CAP = 32
LANES = 128
SUB = 8
HALO = 8
KTILE = 16
GROUP = 32
DEEP = 5
PITCH = 136
MIB = 1024 * 1024


def courant_for(total_lat, spacing):
    coldest = math.cos(0.5 * total_lat * spacing)
    return 0.95 * coldest / math.sqrt(1.0 + coldest * coldest)


def nt(a, b, precision=None):
    return lax.dot_general(
        a, b, (((1,), (1,)), ((), ())), preferred_element_type=jnp.float32, precision=precision
    )


def iota(shape, axis):
    return lax.broadcasted_iota(jnp.int32, shape, axis)


def lanes_between(lane, low, width):
    return (lane >= low) & (lane < low + width)


def rows_kernel(members, eta_ref, dep_ref, sea_ref, first_ref, last_ref, eta, dep, sea, sems):
    rows = eta_ref.shape[1]
    tiles = eta_ref.shape[2] // LANES
    copies = []
    for side, row in ((0, 0), (1, rows - HALO)):
        for k, (src, dst) in enumerate(
            (
                (eta_ref.at[:, pl.ds(row, HALO), :], eta.at[side]),
                (dep_ref.at[pl.ds(row, HALO), :], dep.at[side]),
                (sea_ref.at[pl.ds(row, HALO), :], sea.at[side]),
            )
        ):
            copy = pltpu.make_async_copy(src, dst, sems.at[side, k])
            copy.start()
            copies.append(copy)
    for copy in copies:
        copy.wait()
    for side, out in ((0, first_ref), (1, last_ref)):
        for t in range(tiles):
            at = slice(t * LANES, (t + 1) * LANES)
            wet = sea[side, :, at].astype(jnp.float32)
            for m in range(members):
                out[pl.ds(m * HALO * tiles + t, HALO, stride=tiles), :] = eta[side, m, :, at] * wet
            out[pl.ds(members * HALO * tiles + t, HALO, stride=tiles), :] = dep[side, :, at] * wet


def place_strip(lane, block, west, east):
    base = (block // DEEP) * GROUP
    one = jnp.zeros(lane.shape, jnp.float32)
    two = jnp.zeros(lane.shape, jnp.float32)
    for i in range(len(west)):
        low = base + i * HALO
        here = lanes_between(lane, low, HALO)
        one = jnp.where(here, pltpu.roll(west[i], low, axis=1) if low else west[i], one)
        two = jnp.where(here, pltpu.roll(east[i], (low + HALO) % LANES, axis=1), two)
    return one, two


def table_kernel(
    lat_cells, lon_cells, lat_count, lon_count, members,
    cells_ref, eta_ref, dep_ref, sea_ref, msg_ref, one_ref, two_ref, own_ref, pick_ref, eta, dep, sea, sems,
):
    tiles = lon_cells // LANES
    copies = []
    for side, col in ((0, 0), (1, lon_cells - LANES)):
        for k, (src, dst) in enumerate(
            (
                (eta_ref.at[:, :, pl.ds(col, LANES)], eta.at[side]),
                (dep_ref.at[:, pl.ds(col, LANES)], dep.at[side]),
                (sea_ref.at[:, pl.ds(col, LANES)], sea.at[side]),
            )
        ):
            copy = pltpu.make_async_copy(src, dst, sems.at[side, k])
            copy.start()
            copies.append(copy)

    probes = cells_ref.shape[1]
    rows = cells_ref[0:1, :]
    cols = cells_ref[1:2, :]
    for band in range(lat_count - 1, 0, -1):
        rows = rows - jnp.where(rows >= band * lat_cells, lat_cells, 0)
    sector = jnp.zeros_like(cols)
    for s in range(1, lon_count):
        sector = sector + jnp.where(cols >= s * lon_cells, 1, 0)
    cols = cols - sector * lon_cells
    tile = jnp.zeros_like(cols)
    for t in range(1, tiles):
        tile = tile + jnp.where(cols >= t * LANES, 1, 0)
    lane = cols - tile * LANES
    low = cols < HALO
    high = cols >= lon_cells - HALO
    lane = jnp.where(low, LANES - 2 * HALO + cols, lane)
    lane = jnp.where(high, cols - (lon_cells - 2 * HALO), lane)
    main = (HALO + rows) * tiles + tile
    rim = (lat_cells + 2 * HALO) * tiles + HALO + rows
    place = jnp.where(low | high, rim, main)
    code = (place - HALO * tiles) * LANES + lane
    hits = (iota((lon_count, probes), 0) == sector).astype(jnp.float32)
    before = (iota((probes, probes), 0) < iota((probes, probes), 1)).astype(jnp.float32)
    counts = lax.dot_general(
        hits.astype(jnp.bfloat16),
        before.astype(jnp.bfloat16),
        (((1,), (0,)), ((), ())),
        preferred_element_type=jnp.float32,
    )
    rank = jnp.sum(hits * counts, axis=0, keepdims=True)
    slots = lon_count * CAP
    key = sector * CAP + rank.astype(jnp.int32)
    pick = (iota((slots, probes), 0) == key).astype(jnp.float32).astype(jnp.bfloat16)
    pick_ref[...] = pick
    digit_row = iota((SUB, probes), 0)
    digits = jnp.where(digit_row == 0, code & 255, 0)
    digits = jnp.where(digit_row == 1, (code >> 8) & 255, digits)
    digits = jnp.where(digit_row == 2, code >> 16, digits)
    sent = nt(digits.astype(jnp.float32).astype(jnp.bfloat16), pick)
    sent = (sent[0:1] + 256.0 * sent[1:2] + 65536.0 * sent[2:3]).astype(jnp.int32)
    msg_ref[...] = jnp.zeros_like(msg_ref)
    for s in range(lon_count):
        msg_ref[s, :, 0:CAP] = sent[:, s * CAP : (s + 1) * CAP]

    for copy in copies:
        copy.wait()
    lane = iota((SUB, LANES), 1)
    zero = jnp.zeros((SUB, LANES), jnp.float32)
    total = lat_cells + 2 * HALO
    one = [zero] * DEEP
    two = [zero] * DEEP
    for blk in range(lat_cells // SUB):
        at = slice(blk * SUB, (blk + 1) * SUB)
        wet = [sea[side, at, :].astype(jnp.float32) for side in range(2)]
        west, east = (
            [eta[side, m, at, :] * wet[side] for m in range(members)] + [dep[side, at, :] * wet[side]]
            for side in range(2)
        )
        block = blk + HALO // SUB
        a, b = place_strip(lane, block, west, east)
        here = lanes_between(lane, (block // DEEP) * GROUP, GROUP)
        one[block % DEEP] = jnp.where(here, a, one[block % DEEP])
        two[block % DEEP] = jnp.where(here, b, two[block % DEEP])
        for i in range(members + 1):
            v = jnp.where(lane < 2 * HALO, pltpu.roll(east[i], 2 * HALO, axis=1), 0.0)
            v = jnp.where(lane >= LANES - 2 * HALO, pltpu.roll(west[i], LANES - 2 * HALO, axis=1), v)
            own_ref[i * total + HALO + blk * SUB : i * total + HALO + (blk + 1) * SUB, :] = v
    for d in range(DEEP):
        one_ref[d * SUB : (d + 1) * SUB, :] = one[d]
        two_ref[d * SUB : (d + 1) * SUB, :] = two[d]


def rim_kernel(members, odd_ref, one_ref, two_ref, top_ref, bot_ref, a_ref, b_ref):
    tiles = top_ref.shape[0] // ((members + 1) * HALO)
    lane = iota((SUB, LANES), 1)
    odd = odd_ref[0] == 1
    one = [one_ref[d * SUB : (d + 1) * SUB, :] for d in range(DEEP)]
    two = [two_ref[d * SUB : (d + 1) * SUB, :] for d in range(DEEP)]
    for ref, block in ((top_ref, 0), (bot_ref, DEEP * (LANES // GROUP) - 3)):
        west, east = (
            [ref[pl.ds(i * HALO * tiles + t, HALO, stride=tiles), :] for i in range(members + 1)]
            for t in (0, tiles - 1)
        )
        v, w = place_strip(lane, block, west, east)
        here = lanes_between(lane, (block // DEEP) * GROUP, (members + 1) * HALO)
        d = block % DEEP
        one[d] = jnp.where(here, v, one[d])
        two[d] = jnp.where(here, w, two[d])
    for d in range(DEEP):
        a_ref[d * SUB : (d + 1) * SUB, :] = jnp.where(odd, one[d], two[d])
        b_ref[d * SUB : (d + 1) * SUB, :] = jnp.where(odd, two[d], one[d])


def wave_kernel(
    members, stride, odd_ref, idx_ref, eta_ref, dep_ref, sea_ref, top_ref, bot_ref, a_ref, b_ref, own_ref, fac_ref,
    out_ref, smp_ref, eta, dep, sea, wet, ce, cn, rim_wet, rim_ce, rim_cn, out, sems, out_sems, *rest,
):
    hist = rest[:members]
    east = rest[members : 2 * members]
    north = rest[2 * members : 3 * members]
    rim_east = rest[3 * members : 4 * members]
    rim_north = rest[4 * members : 5 * members]
    rows = eta_ref.shape[1]
    tiles = eta_ref.shape[2] // LANES
    total = rows + 2 * HALO
    blocks = total // SUB
    rim = total * tiles
    lane = iota((SUB, LANES), 1)
    row8 = iota((SUB, LANES), 0)
    last = lane == LANES - 1
    first = lane == 0
    odd = odd_ref[0] == 1
    zero = jnp.zeros((SUB, LANES), jnp.float32)

    copies = []
    for t in range(tiles):
        cols = pl.ds(t * LANES, LANES)
        for m in range(members):
            copies.append((eta_ref.at[m, :, cols], eta.at[pl.ds((m * tiles + t) * PITCH, rows), :]))
        copies.append((dep_ref.at[:, cols], dep.at[pl.ds(t * PITCH, rows), :]))
        copies.append((sea_ref.at[:, cols], sea.at[pl.ds(t * PITCH, rows), :]))
    copies = [pltpu.make_async_copy(a, b, sems.at[k]) for k, (a, b) in enumerate(copies)]
    for copy in copies:
        copy.start()

    def shl(v):
        v = pltpu.roll(v, LANES - 1, axis=1)
        return jnp.where(last, pltpu.roll(v, SUB - 1, axis=0), v)

    def shr(v):
        v = pltpu.roll(v, 1, axis=1)
        return jnp.where(first, pltpu.roll(v, 1, axis=0), v)

    def vec(r):
        return slice(r * tiles, (r + 1) * tiles)

    def blk(b):
        return slice(b * SUB, (b + 1) * SUB)

    def fac(k, r):
        return fac_ref[k * total + r : k * total + r + 1, :]

    for b in range(blocks):
        d = b % DEEP
        base = (b // DEEP) * GROUP
        one = a_ref[blk(d), :]
        two = b_ref[blk(d), :]
        from_left = jnp.where(odd, one, two)
        from_right = jnp.where(odd, two, one)
        for i in range(members + 1):
            if b == 0 or b == blocks - 1:
                ref = top_ref if b == 0 else bot_ref
                w = ref[pl.ds(i * HALO * tiles, HALO, stride=tiles), :]
                e = ref[pl.ds(i * HALO * tiles + tiles - 1, HALO, stride=tiles), :]
                v = jnp.where(lane < 2 * HALO, pltpu.roll(e, 2 * HALO, axis=1), 0.0)
                v = jnp.where(lane >= LANES - 2 * HALO, pltpu.roll(w, LANES - 2 * HALO, axis=1), v)
            else:
                v = own_ref[i * total + b * SUB : i * total + (b + 1) * SUB, :]
            low = base + i * HALO
            far = pltpu.roll(from_right, (2 * HALO - low) % LANES, axis=1)
            v = jnp.where(lanes_between(lane, 2 * HALO, HALO), far, v)
            far = pltpu.roll(from_left, (LANES - 3 * HALO - low) % LANES, axis=1)
            v = jnp.where(lanes_between(lane, LANES - 3 * HALO, HALO), far, v)
            if i < members:
                hist[i][rim + b * SUB : rim + (b + 1) * SUB, :] = v
            else:
                rim_wet[blk(b), :] = v
    rim_wet[blk(blocks), :] = zero
    for q in range(STEPS):
        for m in range(members):
            at = q * stride + rim + total
            hist[m][at : at + SUB, :] = zero
    for b in range(blocks):
        w = rim_wet[blk(b), :]
        below = rim_wet[b * SUB + 1 : (b + 1) * SUB + 1, :]
        rim_ce[blk(b), :] = fac_ref[blk(b), :] * jnp.sqrt(w * pltpu.roll(w, LANES - 1, axis=1))
        rim_cn[blk(b), :] = fac_ref[total + b * SUB : total + (b + 1) * SUB, :] * jnp.sqrt(w * below)

    for ref, row in ((top_ref, 0), (bot_ref, rows + HALO)):
        size = HALO * tiles
        for m in range(members):
            hist[m][row * tiles : row * tiles + size, :] = ref[m * size : (m + 1) * size, :]
        wet[row * tiles : row * tiles + size, :] = ref[members * size : (members + 1) * size, :]
    for copy in copies:
        copy.wait()
    for r in range(rows):
        here = sea[pl.ds(r, tiles, stride=PITCH), :].astype(jnp.float32)
        for m in range(members):
            hist[m][vec(r + HALO), :] = eta[pl.ds(m * tiles * PITCH + r, tiles, stride=PITCH), :] * here
        wet[vec(r + HALO), :] = dep[pl.ds(r, tiles, stride=PITCH), :] * here
    w = wet[vec(0), :]
    for r in range(total - 1):
        below = wet[vec(r + 1), :]
        ce[vec(r), :] = fac(0, r) * jnp.sqrt(w * shl(w))
        cn[vec(r), :] = fac(1, r) * jnp.sqrt(w * below)
        w = below

    for q in range(STEPS):
        low, high = q + 1, total - 1 - q
        base = q * stride
        after = base + stride
        s, above = [], []
        for m in range(members):
            before = hist[m][base + (low - 1) * tiles : base + low * tiles, :]
            s.append(hist[m][base + low * tiles : base + (low + 1) * tiles, :])
            n = s[m] - before
            if q:
                n = north[m][vec(low - 1), :] + n
            above.append(cn[vec(low - 1), :] * n)
        rim_above = [zero] * members

        def rim_block(b):
            scale = fac_ref[2 * total + b * SUB : 2 * total + (b + 1) * SUB, :]
            for m in range(members):
                at = base + rim + b * SUB
                v = hist[m][at : at + SUB, :]
                below = hist[m][at + 1 : at + SUB + 1, :]
                e = pltpu.roll(v, LANES - 1, axis=1) - v
                n = below - v
                if q:
                    e = rim_east[m][blk(b), :] + e
                    n = rim_north[m][blk(b), :] + n
                fe = rim_ce[blk(b), :] * e
                fn = rim_cn[blk(b), :] * n
                if q < STEPS - 1:
                    rim_east[m][blk(b), :] = e
                    rim_north[m][blk(b), :] = n
                moved = pltpu.roll(fn, 1, axis=0)
                upper = jnp.where(row8 == 0, rim_above[m], moved)
                rim_above[m] = moved
                at = at + stride
                hist[m][at : at + SUB, :] = v + ((fe - pltpu.roll(fe, 1, axis=1)) + scale * (fn - upper))

        for r in range(low, high):
            if r % SUB == 0:
                rim_block(r // SUB - 1)
            scale = fac(2, r)
            to_east = ce[vec(r), :]
            to_north = cn[vec(r), :]
            for m in range(members):
                below = hist[m][base + (r + 1) * tiles : base + (r + 2) * tiles, :]
                e = shl(s[m]) - s[m]
                n = below - s[m]
                if q:
                    e = east[m][vec(r), :] + e
                    n = north[m][vec(r), :] + n
                fe = to_east * e
                fn = to_north * n
                if q < STEPS - 1:
                    east[m][vec(r), :] = e
                    north[m][vec(r), :] = n
                hist[m][after + r * tiles : after + (r + 1) * tiles, :] = s[m] + (
                    (fe - shr(fe)) + scale * (fn - above[m])
                )
                s[m] = below
                above[m] = fn
        for b in range((high - 1) // SUB, blocks):
            rim_block(b)

    copies = []
    end = STEPS * stride
    for m in range(members):
        for b in range(rows // SUB):
            at = end + rim + HALO + b * SUB
            edge = hist[m][at : at + SUB, :]
            for t in range(tiles):
                v = hist[m][pl.ds(end + (HALO + b * SUB) * tiles + t, SUB, stride=tiles), :]
                if t == 0:
                    v = jnp.where(lane < HALO, pltpu.roll(edge, 2 * HALO, axis=1), v)
                if t == tiles - 1:
                    v = jnp.where(lane >= LANES - HALO, pltpu.roll(edge, LANES - 2 * HALO, axis=1), v)
                out[m, blk(b), t * LANES : (t + 1) * LANES] = v
        copy = pltpu.make_async_copy(out.at[m], out_ref.at[m], out_sems.at[m])
        copy.start()
        copies.append(copy)

    def sample(s, carry):
        acc = zero
        for j in range(CAP):
            code = idx_ref[s, 0, j]
            spot = lax.bitwise_and(code, LANES - 1)
            place = lax.shift_right_logical(code, 7) + (stride + HALO * tiles)
            for m in range(members):
                v = hist[m][pl.ds(place, STEPS, stride=stride), :]
                target = m * CAP + j
                v = pltpu.roll(v, lax.bitwise_and(target - spot, LANES - 1), axis=1)
                acc = jnp.where(lane == target, v, acc)
        smp_ref[s] = acc
        return carry

    lax.fori_loop(0, smp_ref.shape[0], sample, 0)
    for copy in copies:
        copy.wait()


def past_kernel(members, g_ref, e_ref, out_ref, g, e, sems):
    coast, probes, lag_count = g_ref.shape[1:]
    parts = probes // KTILE
    copies = [pltpu.make_async_copy(e_ref.at[0], e, sems.at[parts])]
    for k in range(parts):
        at = pl.ds(k * KTILE, KTILE)
        copies.append(pltpu.make_async_copy(g_ref.at[0, :, at, :], g.at[k], sems.at[k]))
    for copy in copies:
        copy.start()
    copies[0].wait()
    lane = iota((members * KTILE, LANES), 1)

    def windows(k):
        past = e[:, k * KTILE : (k + 1) * KTILE, :].reshape(members * KTILE, lag_count).astype(jnp.float32)
        shifted = []
        for t in range(1, STEPS + 1):
            moved = pltpu.roll(past, t, axis=1)
            start = jnp.where(lane >= t, moved[:, :LANES], 0.0)
            shifted.append(jnp.concatenate([start, moved[:, LANES:]], axis=1).astype(jnp.bfloat16))
        return jnp.concatenate(shifted, axis=0)

    acc = None
    for k in range(0, parts, 2):
        w = jnp.concatenate([windows(k), windows(k + 1)], axis=1)
        copies[1 + k].wait()
        copies[2 + k].wait()
        x = jnp.concatenate([g[k + i].reshape(coast * KTILE, lag_count) for i in range(2)], axis=1)
        part = nt(x, w)
        acc = part if acc is None else acc + part
    same = (iota(acc.shape, 0) & (KTILE - 1)) == (iota(acc.shape, 1) & (KTILE - 1))
    kept = jnp.sum(jnp.where(same, acc, 0.0).reshape(coast, KTILE, acc.shape[1]), axis=1)
    wins = members * STEPS
    row = iota((wins, acc.shape[1]), 0)
    col = iota((wins, acc.shape[1]), 1)
    fold = ((col // KTILE) == (row & (STEPS - 1)) * members + row // STEPS).astype(jnp.float32)
    out_ref[...] = nt(fold, kept, precision=lax.Precision.HIGHEST)


def recent_kernel(g_ref, pick_ref, out_ref, lags_ref):
    coast = g_ref.shape[0]
    probes = g_ref.shape[1]
    first = (iota((SUB, LANES), 0) == iota((SUB, LANES), 1)).astype(jnp.float32).astype(jnp.bfloat16)
    for c in range(coast):
        lags_ref[c * SUB : (c + 1) * SUB, :] = nt(first, g_ref[c])
    size = coast * SUB
    r = iota((size, size), 0)
    q = iota((size, size), 1)
    order = ((r & (coast - 1)) == (q >> 3)) & ((r // coast) == (q & 7))
    order = order.astype(jnp.float32).astype(jnp.bfloat16)
    lags = lax.dot_general(
        order,
        lags_ref[...].astype(jnp.bfloat16),
        (((1,), (0,)), ((), ())),
        preferred_element_type=jnp.float32,
    )
    out_ref[...] = nt(lags.astype(jnp.bfloat16), pick_ref[...]).astype(jnp.bfloat16)


def shore_kernel(members, rec_ref, gp_ref, prior_ref, out_ref):
    lon_count = rec_ref.shape[0]
    coast = out_ref.shape[1]
    per = LANES // CAP
    lane = iota((SUB, LANES), 1)
    series = []
    for m in range(members):
        row = []
        for tile in range(lon_count // per):
            acc = jnp.zeros((SUB, LANES), jnp.float32)
            for j in range(per):
                v = pltpu.roll(rec_ref[tile * per + j], ((j - m) * CAP) % LANES, axis=1)
                acc = jnp.where((lane >= j * CAP) & (lane < (j + 1) * CAP), v, acc)
            row.append(acc)
        series.append(jnp.concatenate(row, axis=1))
    x = jnp.concatenate(series, axis=0)
    hi = x.astype(jnp.bfloat16)
    rest = x - hi.astype(jnp.float32)
    mid = rest.astype(jnp.bfloat16)
    lo = (rest - mid.astype(jnp.float32)).astype(jnp.bfloat16)
    r = nt(jnp.concatenate([hi, mid, lo], axis=0), gp_ref[...])
    n = members * STEPS
    r = r[0:n] + r[n : 2 * n] + r[2 * n : 3 * n]
    row8 = iota((SUB, LANES), 0)
    per = LANES // coast
    for m in range(members):
        total = jnp.zeros((SUB, LANES), jnp.float32)
        for l in range(STEPS):
            v = r[m * SUB : (m + 1) * SUB, (l // per) * LANES : (l // per + 1) * LANES]
            if l % per:
                v = pltpu.roll(v, LANES - (l % per) * coast, axis=1)
            if l:
                v = jnp.where(row8 >= l, pltpu.roll(v, l, axis=0), 0.0)
            total = total + v
        out_ref[m * SUB : (m + 1) * SUB, :] = prior_ref[m * SUB : (m + 1) * SUB, :] + total[:, 0:coast]


def local(eta_init, depth, sea_mask, probe_cells, elapsed_record, gauge_kernels):
    members, lat_cells, lon_cells = eta_init.shape
    lat_count = lax.axis_size("lat")
    lon_count = lax.axis_size("lon")
    coast, probes, lag_count = gauge_kernels.shape[1:]
    total_lat = lat_cells * lat_count
    total_lon = lon_cells * lon_count
    spacing = 2.0 * math.pi / total_lon
    courant = courant_for(total_lat, spacing)
    tiles = lon_cells // LANES
    total = lat_cells + 2 * HALO
    stride = total * tiles + total + SUB
    slots = lon_count * CAP
    f32 = jnp.float32
    vmem = pl.BlockSpec(memory_space=pltpu.VMEM)
    smem = pl.BlockSpec(memory_space=pltpu.SMEM)
    hbm = pl.BlockSpec(memory_space=pltpu.HBM)
    dma = pltpu.SemaphoreType.DMA

    def limit(mib):
        return pltpu.CompilerParams(vmem_limit_bytes=mib * MIB)

    def cost(us):
        return pl.CostEstimate(flops=0, bytes_accessed=int(us * 3.0e6), transcendentals=0)

    def stay(*arrays):
        return [pltpu.with_memory_space_constraint(a, pltpu.HBM) for a in arrays]

    halo_shape = jax.ShapeDtypeStruct(((members + 1) * HALO * tiles, LANES), f32)
    first_rows, last_rows = pl.pallas_call(
        functools.partial(rows_kernel, members),
        out_shape=[halo_shape] * 2,
        in_specs=[hbm] * 3,
        out_specs=[vmem] * 2,
        scratch_shapes=[
            pltpu.VMEM((2, members, HALO, lon_cells), f32),
            pltpu.VMEM((2, HALO, lon_cells), f32),
            pltpu.VMEM((2, HALO, lon_cells), jnp.int32),
            dma((2, 3)),
        ],
        compiler_params=limit(8),
        cost_estimate=cost(1),
        name="rows",
    )(*stay(eta_init, depth, sea_mask))
    up = [(i, i + 1) for i in range(lat_count - 1)]
    down = [(i + 1, i) for i in range(lat_count - 1)]
    top = lax.ppermute(last_rows, "lat", up)
    bottom = lax.ppermute(first_rows, "lat", down)

    first_row = lax.axis_index("lat") * lat_cells - HALO
    ids = (first_row + jnp.arange(total, dtype=jnp.int32)).astype(f32)
    latitude = -0.5 * total_lat * spacing + (ids + 0.5) * spacing
    scale = courant / jnp.cos(latitude)
    factors = jnp.stack([scale * scale, courant * jnp.cos(latitude + 0.5 * spacing), scale])
    factors = jnp.broadcast_to(factors[:, :, None], (3, total, LANES)).reshape(3 * total, LANES)

    strip = jax.ShapeDtypeStruct((DEEP * SUB, LANES), f32)
    sent, one, two, own, pick = pl.pallas_call(
        functools.partial(table_kernel, lat_cells, lon_cells, lat_count, lon_count, members),
        out_shape=[
            jax.ShapeDtypeStruct((lon_count, 1, LANES), jnp.int32),
            strip,
            strip,
            jax.ShapeDtypeStruct(((members + 1) * total, LANES), f32),
            jax.ShapeDtypeStruct((slots, probes), jnp.bfloat16),
        ],
        in_specs=[vmem, hbm, hbm, hbm],
        out_specs=[vmem] * 5,
        scratch_shapes=[
            pltpu.VMEM((2, members, lat_cells, LANES), f32),
            pltpu.VMEM((2, lat_cells, LANES), f32),
            pltpu.VMEM((2, lat_cells, LANES), jnp.int32),
            dma((2, 3)),
        ],
        compiler_params=limit(8),
        cost_estimate=cost(1.5),
        name="table",
    )(probe_cells[0], *stay(eta_init, depth, sea_mask))
    incoming = lax.all_to_all(sent, "lon", split_axis=0, concat_axis=0, tiled=True)

    recent = pl.pallas_call(
        recent_kernel,
        grid=(1,),
        out_shape=jax.ShapeDtypeStruct((STEPS * coast, slots), jnp.bfloat16),
        in_specs=[
            pl.BlockSpec((None, coast, probes, LANES), lambda k: (0, 0, 0, 0)),
            pl.BlockSpec((slots, probes), lambda k: (0, 0)),
        ],
        out_specs=pl.BlockSpec((STEPS * coast, slots), lambda k: (0, 0)),
        scratch_shapes=[pltpu.VMEM((STEPS * coast, probes), f32)],
        compiler_params=limit(12),
        cost_estimate=cost(2.5),
        name="recent",
    )(*stay(gauge_kernels), pick)

    odd = lax.rem(lax.axis_index("lon"), 2).astype(jnp.int32)[None]
    send_a, send_b = pl.pallas_call(
        functools.partial(rim_kernel, members),
        out_shape=[strip] * 2,
        in_specs=[smem] + [vmem] * 4,
        out_specs=[vmem] * 2,
        compiler_params=limit(8),
        cost_estimate=cost(0.5),
        name="rim",
    )(odd, one, two, top, bottom)
    swap_a = [(i, i ^ 1) for i in range(lon_count)]
    swap_b = [((i + 1) % lon_count, ((i ^ 1) + 1) % lon_count) for i in range(lon_count)]
    rim_a = lax.ppermute(send_a, "lon", swap_a)
    rim_b = lax.ppermute(send_b, "lon", swap_b)

    field = pltpu.VMEM((total * tiles, LANES), f32)
    tall = pltpu.VMEM((total + SUB, LANES), f32)
    eta_final, samples = pl.pallas_call(
        functools.partial(wave_kernel, members, stride),
        out_shape=[
            jax.ShapeDtypeStruct(eta_init.shape, f32),
            jax.ShapeDtypeStruct((lon_count, SUB, LANES), f32),
        ],
        in_specs=[smem] * 2 + [hbm] * 3 + [vmem] * 6,
        out_specs=[hbm, vmem],
        scratch_shapes=[
            pltpu.VMEM((members * tiles * PITCH, LANES), f32),
            pltpu.VMEM((tiles * PITCH, LANES), f32),
            pltpu.VMEM((tiles * PITCH, LANES), jnp.int32),
            field,
            field,
            field,
            tall,
            tall,
            tall,
            pltpu.VMEM(eta_init.shape, f32),
            dma(((members + 2) * tiles,)),
            dma((members,)),
        ]
        + [pltpu.VMEM(((STEPS + 1) * stride, LANES), f32)] * members
        + [field] * (2 * members)
        + [tall] * (2 * members),
        compiler_params=limit(32),
        cost_estimate=cost(11),
        name="wave",
    )(odd, incoming, *stay(eta_init, depth, sea_mask), top, bottom, rim_a, rim_b, own, factors)

    answered = lax.all_to_all(samples, "lon", split_axis=0, concat_axis=0, tiled=True)
    prior = pl.pallas_call(
        functools.partial(past_kernel, members),
        out_shape=jax.ShapeDtypeStruct((members * STEPS, coast), f32),
        in_specs=[hbm, hbm],
        out_specs=vmem,
        scratch_shapes=[
            pltpu.VMEM((probes // KTILE, coast, KTILE, lag_count), jnp.bfloat16),
            pltpu.VMEM((members, probes, lag_count), jnp.bfloat16),
            dma((probes // KTILE + 1,)),
        ],
        compiler_params=limit(28),
        cost_estimate=cost(6),
        name="past",
    )(*stay(gauge_kernels, elapsed_record))
    shore = pl.pallas_call(
        functools.partial(shore_kernel, members),
        out_shape=jax.ShapeDtypeStruct((members * STEPS, coast), f32),
        in_specs=[vmem, vmem, vmem],
        out_specs=vmem,
        compiler_params=limit(8),
        cost_estimate=cost(1),
        name="shore",
    )(answered, recent, prior)
    return eta_final, shore.reshape(1, members, STEPS, coast)


def solution(mesh):
    in_specs = (
        P(None, "lat", "lon"),
        P("lat", "lon"),
        P("lat", "lon"),
        P(("lon", "lat"), None, None),
        P(("lon", "lat"), None, None, None),
        P(("lon", "lat"), None, None, None),
    )
    out_specs = (P(None, "lat", "lon"), P(("lon", "lat"), None, None, None))
    return jax.shard_map(local, mesh=mesh, in_specs=in_specs, out_specs=out_specs, check_vma=False)
```

```python
import functools
import math

import jax
import jax.numpy as jnp
from jax import lax
from jax.experimental import pallas as pl
from jax.experimental.pallas import tpu as pltpu
from jax.sharding import PartitionSpec as P

STEPS = 8
CAP = 32
LANES = 128
SUB = 8
HALO = 8
KTILE = 16
GROUP = 32
DEEP = 5
PARTS = 4
MIB = 1024 * 1024


def courant_for(total_lat, spacing):
    coldest = math.cos(0.5 * total_lat * spacing)
    return 0.95 * coldest / math.sqrt(1.0 + coldest * coldest)


def nt(a, b, precision=None):
    return lax.dot_general(
        a, b, (((1,), (1,)), ((), ())), preferred_element_type=jnp.float32, precision=precision
    )


def iota(shape, axis):
    return lax.broadcasted_iota(jnp.int32, shape, axis)


def lanes_between(lane, low, width):
    return (lane >= low) & (lane < low + width)


def rows_kernel(members, eta_ref, dep_ref, sea_ref, first_ref, last_ref, eta, dep, sea, sems):
    rows = eta_ref.shape[1]
    tiles = eta_ref.shape[2] // LANES
    copies = []
    for side, row in ((0, 0), (1, rows - HALO)):
        for k, (src, dst) in enumerate(
            (
                (eta_ref.at[:, pl.ds(row, HALO), :], eta.at[side]),
                (dep_ref.at[pl.ds(row, HALO), :], dep.at[side]),
                (sea_ref.at[pl.ds(row, HALO), :], sea.at[side]),
            )
        ):
            copy = pltpu.make_async_copy(src, dst, sems.at[side, k])
            copy.start()
            copies.append(copy)
    for copy in copies:
        copy.wait()
    for side, out in ((0, first_ref), (1, last_ref)):
        for t in range(tiles):
            at = slice(t * LANES, (t + 1) * LANES)
            wet = sea[side, :, at].astype(jnp.float32)
            for m in range(members):
                out[pl.ds(m * HALO * tiles + t, HALO, stride=tiles), :] = eta[side, m, :, at] * wet
            out[pl.ds(members * HALO * tiles + t, HALO, stride=tiles), :] = dep[side, :, at] * wet


def place_strip(lane, block, west, east):
    base = (block // DEEP) * GROUP
    one = jnp.zeros(lane.shape, jnp.float32)
    two = jnp.zeros(lane.shape, jnp.float32)
    for i in range(len(west)):
        low = base + i * HALO
        here = lanes_between(lane, low, HALO)
        one = jnp.where(here, pltpu.roll(west[i], low, axis=1) if low else west[i], one)
        two = jnp.where(here, pltpu.roll(east[i], (low + HALO) % LANES, axis=1), two)
    return one, two


def table_kernel(
    lat_cells, lon_cells, lat_count, lon_count, members,
    cells_ref, eta_ref, dep_ref, sea_ref, msg_ref, one_ref, two_ref, own_ref, pick_ref, eta, dep, sea, cells, sems, cell_sem,
):
    tiles = lon_cells // LANES
    table = pltpu.make_async_copy(cells_ref.at[0], cells, cell_sem.at[0])
    table.start()
    copies = []
    for side, col in ((0, 0), (1, lon_cells - LANES)):
        for k, (src, dst) in enumerate(
            (
                (eta_ref.at[:, :, pl.ds(col, LANES)], eta.at[side]),
                (dep_ref.at[:, pl.ds(col, LANES)], dep.at[side]),
                (sea_ref.at[:, pl.ds(col, LANES)], sea.at[side]),
            )
        ):
            copy = pltpu.make_async_copy(src, dst, sems.at[side, k])
            copy.start()
            copies.append(copy)

    probes = cells.shape[1]
    table.wait()
    rows = cells[0:1, :]
    cols = cells[1:2, :]
    for band in range(lat_count - 1, 0, -1):
        rows = rows - jnp.where(rows >= band * lat_cells, lat_cells, 0)
    sector = jnp.zeros_like(cols)
    for s in range(1, lon_count):
        sector = sector + jnp.where(cols >= s * lon_cells, 1, 0)
    cols = cols - sector * lon_cells
    tile = jnp.zeros_like(cols)
    for t in range(1, tiles):
        tile = tile + jnp.where(cols >= t * LANES, 1, 0)
    lane = cols - tile * LANES
    low = cols < HALO
    high = cols >= lon_cells - HALO
    lane = jnp.where(low, LANES - 2 * HALO + cols, lane)
    lane = jnp.where(high, cols - (lon_cells - 2 * HALO), lane)
    main = (HALO + rows) * tiles + tile
    rim = (lat_cells + 2 * HALO) * tiles + HALO + rows
    place = jnp.where(low | high, rim, main)
    code = (place - HALO * tiles) * LANES + lane
    hits = (iota((lon_count, probes), 0) == sector).astype(jnp.float32)
    before = (iota((probes, probes), 0) < iota((probes, probes), 1)).astype(jnp.float32)
    counts = lax.dot_general(
        hits.astype(jnp.bfloat16),
        before.astype(jnp.bfloat16),
        (((1,), (0,)), ((), ())),
        preferred_element_type=jnp.float32,
    )
    rank = jnp.sum(hits * counts, axis=0, keepdims=True)
    slots = lon_count * CAP
    key = sector * CAP + rank.astype(jnp.int32)
    pick = (iota((slots, probes), 0) == key).astype(jnp.float32).astype(jnp.bfloat16)
    pick_ref[...] = pick
    digit_row = iota((SUB, probes), 0)
    digits = jnp.where(digit_row == 0, code & 255, 0)
    digits = jnp.where(digit_row == 1, (code >> 8) & 255, digits)
    digits = jnp.where(digit_row == 2, code >> 16, digits)
    sent = nt(digits.astype(jnp.float32).astype(jnp.bfloat16), pick)
    sent = (sent[0:1] + 256.0 * sent[1:2] + 65536.0 * sent[2:3]).astype(jnp.int32)
    msg_ref[...] = jnp.zeros_like(msg_ref)
    for s in range(lon_count):
        msg_ref[s, :, 0:CAP] = sent[:, s * CAP : (s + 1) * CAP]

    for copy in copies:
        copy.wait()
    lane = iota((SUB, LANES), 1)
    zero = jnp.zeros((SUB, LANES), jnp.float32)
    total = lat_cells + 2 * HALO
    one = [zero] * DEEP
    two = [zero] * DEEP
    for blk in range(lat_cells // SUB):
        at = slice(blk * SUB, (blk + 1) * SUB)
        wet = [sea[side, at, :].astype(jnp.float32) for side in range(2)]
        west, east = (
            [eta[side, m, at, :] * wet[side] for m in range(members)] + [dep[side, at, :] * wet[side]]
            for side in range(2)
        )
        block = blk + HALO // SUB
        a, b = place_strip(lane, block, west, east)
        here = lanes_between(lane, (block // DEEP) * GROUP, GROUP)
        one[block % DEEP] = jnp.where(here, a, one[block % DEEP])
        two[block % DEEP] = jnp.where(here, b, two[block % DEEP])
        for i in range(members + 1):
            v = jnp.where(lane < 2 * HALO, pltpu.roll(east[i], 2 * HALO, axis=1), 0.0)
            v = jnp.where(lane >= LANES - 2 * HALO, pltpu.roll(west[i], LANES - 2 * HALO, axis=1), v)
            own_ref[i * total + HALO + blk * SUB : i * total + HALO + (blk + 1) * SUB, :] = v
    for d in range(DEEP):
        one_ref[d * SUB : (d + 1) * SUB, :] = one[d]
        two_ref[d * SUB : (d + 1) * SUB, :] = two[d]


def rim_kernel(members, odd_ref, one_ref, two_ref, top_ref, bot_ref, a_ref, b_ref):
    tiles = top_ref.shape[0] // ((members + 1) * HALO)
    lane = iota((SUB, LANES), 1)
    odd = jnp.broadcast_to(odd_ref[...], (SUB, LANES)) == 1
    one = [one_ref[d * SUB : (d + 1) * SUB, :] for d in range(DEEP)]
    two = [two_ref[d * SUB : (d + 1) * SUB, :] for d in range(DEEP)]
    for ref, block in ((top_ref, 0), (bot_ref, DEEP * (LANES // GROUP) - 3)):
        west, east = (
            [ref[pl.ds(i * HALO * tiles + t, HALO, stride=tiles), :] for i in range(members + 1)]
            for t in (0, tiles - 1)
        )
        v, w = place_strip(lane, block, west, east)
        here = lanes_between(lane, (block // DEEP) * GROUP, (members + 1) * HALO)
        d = block % DEEP
        one[d] = jnp.where(here, v, one[d])
        two[d] = jnp.where(here, w, two[d])
    for d in range(DEEP):
        a_ref[d * SUB : (d + 1) * SUB, :] = jnp.where(odd, one[d], two[d])
        b_ref[d * SUB : (d + 1) * SUB, :] = jnp.where(odd, two[d], one[d])


def wave_kernel(
    members, stride, odd_ref, idx_ref, _, pick_ref, eta_ref, dep_ref, sea_ref, g_ref, top_ref, bot_ref, a_ref, b_ref, own_ref, fac_ref,
    out_ref, smp_ref, gp_ref, eta, dep, sea, wet, ce, cw, cn, rim_wet, rim_ce, rim_cn, out, places, taps, lags, sems, out_sems, idx_sem, *rest,
):
    hist = rest[:members]
    past = rest[members : 2 * members]
    rim_east = rest[2 * members : 3 * members]
    rim_north = rest[3 * members : 4 * members]
    rows = eta_ref.shape[1]
    tiles = eta_ref.shape[2] // LANES
    total = rows + 2 * HALO
    blocks = total // SUB
    rim = total * tiles
    lane = iota((SUB, LANES), 1)
    row8 = iota((SUB, LANES), 0)
    last = lane == LANES - 1
    first = lane == 0
    odd = jnp.broadcast_to(odd_ref[...], (SUB, LANES)) == 1
    zero = jnp.zeros((SUB, LANES), jnp.float32)

    part = rows // PARTS
    arriving = []
    for k in range(PARTS):
        at = pl.ds(k * part, part)
        arriving.append(
            [
                pltpu.make_async_copy(eta_ref.at[:, at, :], eta.at[:, at, :], sems.at[k, 0]),
                pltpu.make_async_copy(dep_ref.at[at, :], dep.at[at, :], sems.at[k, 1]),
                pltpu.make_async_copy(sea_ref.at[at, :], sea.at[at, :], sems.at[k, 2]),
            ]
        )
        for copy in arriving[k]:
            copy.start()
    to_scalar = pltpu.make_async_copy(idx_ref, places, idx_sem.at[0])
    to_scalar.start()
    tapped = pltpu.make_async_copy(g_ref.at[0, :, :, pl.ds(0, LANES)], taps, idx_sem.at[1])
    tapped.start()
    coast = taps.shape[0]

    def shl(v):
        v = pltpu.roll(v, LANES - 1, axis=1)
        return jnp.where(last, pltpu.roll(v, SUB - 1, axis=0), v)

    def shr(v):
        v = pltpu.roll(v, 1, axis=1)
        return jnp.where(first, pltpu.roll(v, 1, axis=0), v)

    def vec(r):
        return slice(r * tiles, (r + 1) * tiles)

    def blk(b):
        return slice(b * SUB, (b + 1) * SUB)

    def fac(k, r):
        return fac_ref[k * total + r : k * total + r + 1, :]

    for b in range(blocks):
        d = b % DEEP
        base = (b // DEEP) * GROUP
        one = a_ref[blk(d), :]
        two = b_ref[blk(d), :]
        from_left = jnp.where(odd, one, two)
        from_right = jnp.where(odd, two, one)
        for i in range(members + 1):
            if b == 0 or b == blocks - 1:
                ref = top_ref if b == 0 else bot_ref
                w = ref[pl.ds(i * HALO * tiles, HALO, stride=tiles), :]
                e = ref[pl.ds(i * HALO * tiles + tiles - 1, HALO, stride=tiles), :]
                v = jnp.where(lane < 2 * HALO, pltpu.roll(e, 2 * HALO, axis=1), 0.0)
                v = jnp.where(lane >= LANES - 2 * HALO, pltpu.roll(w, LANES - 2 * HALO, axis=1), v)
            else:
                v = own_ref[i * total + b * SUB : i * total + (b + 1) * SUB, :]
            low = base + i * HALO
            far = pltpu.roll(from_right, (2 * HALO - low) % LANES, axis=1)
            v = jnp.where(lanes_between(lane, 2 * HALO, HALO), far, v)
            far = pltpu.roll(from_left, (LANES - 3 * HALO - low) % LANES, axis=1)
            v = jnp.where(lanes_between(lane, LANES - 3 * HALO, HALO), far, v)
            if i < members:
                hist[i][rim + b * SUB : rim + (b + 1) * SUB, :] = v
            else:
                rim_wet[blk(b), :] = v
    rim_wet[blk(blocks), :] = zero
    for q in range(STEPS):
        for m in range(members):
            at = q * stride + rim + total
            hist[m][at : at + SUB, :] = zero
    for b in range(blocks):
        w = rim_wet[blk(b), :]
        below = rim_wet[b * SUB + 1 : (b + 1) * SUB + 1, :]
        rim_ce[blk(b), :] = fac_ref[blk(b), :] * jnp.sqrt(w * pltpu.roll(w, LANES - 1, axis=1))
        rim_cn[blk(b), :] = fac_ref[total + b * SUB : total + (b + 1) * SUB, :] * jnp.sqrt(w * below)

    for ref, row in ((top_ref, 0), (bot_ref, rows + HALO)):
        size = HALO * tiles
        for m in range(members):
            hist[m][row * tiles : row * tiles + size, :] = ref[m * size : (m + 1) * size, :]
        wet[row * tiles : row * tiles + size, :] = ref[members * size : (members + 1) * size, :]
    done = 0
    for k in range(PARTS):
        for copy in arriving[k]:
            copy.wait()
        for b in range(k * part // SUB, (k + 1) * part // SUB):
            for t in range(tiles):
                cols = slice(t * LANES, (t + 1) * LANES)
                at = pl.ds((HALO + b * SUB) * tiles + t, SUB, stride=tiles)
                here = sea[blk(b), cols].astype(jnp.float32)
                for m in range(members):
                    hist[m][at, :] = eta[m, blk(b), cols] * here
                wet[at, :] = dep[blk(b), cols] * here
        ready = total - 1 if k == PARTS - 1 else HALO + (k + 1) * part - 1
        w = wet[vec(done), :]
        for r in range(done, ready):
            below = wet[vec(r + 1), :]
            edge = fac(0, r) * jnp.sqrt(w * shl(w))
            ce[vec(r), :] = edge
            cw[vec(r), :] = shr(edge)
            cn[vec(r), :] = fac(1, r) * jnp.sqrt(w * below)
            w = below
        done = ready

    leaving = []
    end = STEPS * stride

    def finish(b):
        for m in range(members):
            at = end + rim + HALO + b * SUB
            edge = hist[m][at : at + SUB, :]
            for t in range(tiles):
                v = hist[m][pl.ds(end + (HALO + b * SUB) * tiles + t, SUB, stride=tiles), :]
                if t == 0:
                    v = jnp.where(lane < HALO, pltpu.roll(edge, 2 * HALO, axis=1), v)
                if t == tiles - 1:
                    v = jnp.where(lane >= LANES - HALO, pltpu.roll(edge, LANES - 2 * HALO, axis=1), v)
                out[m, blk(b), t * LANES : (t + 1) * LANES] = v
        if (b + 1) * SUB % part == 0:
            k = (b + 1) * SUB // part - 1
            at = pl.ds(k * part, part)
            copy = pltpu.make_async_copy(out.at[:, at, :], out_ref.at[:, at, :], out_sems.at[k])
            copy.start()
            leaving.append(copy)

    def read_taps(c):
        unit = (iota((SUB, LANES), 0) == iota((SUB, LANES), 1)).astype(jnp.float32).astype(jnp.bfloat16)
        lags[c * SUB : (c + 1) * SUB, :] = nt(unit, taps[c])

    def sort_taps():
        size = coast * SUB
        r = iota((size, size), 0)
        c = iota((size, size), 1)
        order = ((r & (coast - 1)) == (c >> 3)) & ((r // coast) == (c & 7))
        ordered = lax.dot_general(
            order.astype(jnp.float32).astype(jnp.bfloat16),
            lags[...].astype(jnp.bfloat16),
            (((1,), (0,)), ((), ())),
            preferred_element_type=jnp.float32,
        )
        gp_ref[...] = nt(ordered.astype(jnp.bfloat16), pick_ref[...]).astype(jnp.bfloat16)

    for q in range(STEPS):
        low, high = q + 1, total - 1 - q
        base = q * stride
        after = base + stride
        s, sums, above = [], [], []

        def summed(m, r, v):
            if q == 0:
                return v
            old = hist[m][vec(r), :] if q == 1 else past[m][vec(r), :]
            new = old + v
            if q < STEPS - 1:
                past[m][vec(r), :] = new
            return new

        for m in range(members):
            before = summed(m, low - 1, hist[m][base + (low - 1) * tiles : base + low * tiles, :])
            s.append(hist[m][base + low * tiles : base + (low + 1) * tiles, :])
            sums.append(summed(m, low, s[m]))
            above.append(cn[vec(low - 1), :] * (sums[m] - before))
        rim_above = [zero] * members

        def rim_block(b):
            scale = fac_ref[2 * total + b * SUB : 2 * total + (b + 1) * SUB, :]
            for m in range(members):
                at = base + rim + b * SUB
                v = hist[m][at : at + SUB, :]
                below = hist[m][at + 1 : at + SUB + 1, :]
                e = pltpu.roll(v, LANES - 1, axis=1) - v
                n = below - v
                if q:
                    e = rim_east[m][blk(b), :] + e
                    n = rim_north[m][blk(b), :] + n
                fe = rim_ce[blk(b), :] * e
                fn = rim_cn[blk(b), :] * n
                if q < STEPS - 1:
                    rim_east[m][blk(b), :] = e
                    rim_north[m][blk(b), :] = n
                moved = pltpu.roll(fn, 1, axis=0)
                upper = jnp.where(row8 == 0, rim_above[m], moved)
                rim_above[m] = moved
                at = at + stride
                hist[m][at : at + SUB, :] = v + ((fe - pltpu.roll(fe, 1, axis=1)) + scale * (fn - upper))

        for r in range(low, high):
            if r % SUB == 0:
                rim_block(r // SUB - 1)
            if q == 2 and r % 4 == 0 and r // 4 <= coast:
                if r == 4:
                    tapped.wait()
                read_taps(r // 4 - 1)
            if q == 4 and r == rows // 2:
                sort_taps()
            scale = fac(2, r)
            to_east = ce[vec(r), :]
            to_west = cw[vec(r), :]
            to_north = cn[vec(r), :]
            for m in range(members):
                below = hist[m][base + (r + 1) * tiles : base + (r + 2) * tiles, :]
                sum_below = summed(m, r + 1, below)
                pulled = to_east * (shl(sums[m]) - sums[m]) - to_west * (sums[m] - shr(sums[m]))
                fn = to_north * (sum_below - sums[m])
                hist[m][after + r * tiles : after + (r + 1) * tiles, :] = s[m] + (
                    pulled + scale * (fn - above[m])
                )
                s[m] = below
                sums[m] = sum_below
                above[m] = fn
            if q == STEPS - 1 and r % SUB == SUB - 1 and r >= HALO + 2 * SUB - 1:
                finish((r - HALO) // SUB - 1)
        for b in range((high - 1) // SUB, blocks):
            rim_block(b)
    finish(rows // SUB - 1)

    def sample(s, carry):
        acc = zero
        for j in range(CAP):
            code = places[s, 0, j]
            spot = lax.bitwise_and(code, LANES - 1)
            place = lax.shift_right_logical(code, 7) + (stride + HALO * tiles)
            for m in range(members):
                v = hist[m][pl.ds(place, STEPS, stride=stride), :]
                target = m * CAP + j
                v = pltpu.roll(v, lax.bitwise_and(target - spot, LANES - 1), axis=1)
                acc = jnp.where(lane == target, v, acc)
        smp_ref[s] = acc
        return carry

    to_scalar.wait()
    lax.fori_loop(0, smp_ref.shape[0], sample, 0)
    for copy in leaving:
        copy.wait()


def past_kernel(members, g_ref, e_ref, _, out_ref, acc_ref):
    coast, probes, lag_count = g_ref.shape
    step = pl.program_id(0)
    lane = iota((members * KTILE, LANES), 1)
    rows = []
    windows = []
    for k in range(probes // KTILE):
        at = slice(k * KTILE, (k + 1) * KTILE)
        past = e_ref[:, at, :].reshape(members * KTILE, lag_count).astype(jnp.float32)
        shifted = []
        for t in range(1, STEPS + 1):
            moved = pltpu.roll(past, t, axis=1)
            start = jnp.where(lane >= t, moved[:, :LANES], 0.0)
            shifted.append(jnp.concatenate([start, moved[:, LANES:]], axis=1).astype(jnp.bfloat16))
        windows.append(jnp.concatenate(shifted, axis=0))
        rows.append(g_ref[:, at, :].reshape(coast * KTILE, lag_count))
    part = nt(jnp.concatenate(rows, axis=1), jnp.concatenate(windows, axis=1))

    @pl.when(step == 0)
    def _():
        acc_ref[...] = part

    @pl.when(step > 0)
    def _():
        acc_ref[...] += part

    @pl.when(step == pl.num_programs(0) - 1)
    def _():
        acc = acc_ref[...]
        same = (iota(acc.shape, 0) & (KTILE - 1)) == (iota(acc.shape, 1) & (KTILE - 1))
        kept = jnp.sum(jnp.where(same, acc, 0.0).reshape(coast, KTILE, acc.shape[1]), axis=1)
        wins = members * STEPS
        row = iota((wins, acc.shape[1]), 0)
        col = iota((wins, acc.shape[1]), 1)
        fold = ((col // KTILE) == (row & (STEPS - 1)) * members + row // STEPS).astype(jnp.float32)
        out_ref[...] = nt(fold, kept, precision=lax.Precision.HIGHEST)


def shore_kernel(members, rec_ref, gp_ref, prior_ref, few_ref, out_ref):
    lon_count = rec_ref.shape[0]
    coast = out_ref.shape[1]
    per = LANES // CAP
    lane = iota((SUB, LANES), 1)
    series = []
    for m in range(members):
        row = []
        for tile in range(lon_count // per):
            acc = jnp.zeros((SUB, LANES), jnp.float32)
            for j in range(per):
                v = pltpu.roll(rec_ref[tile * per + j], ((j - m) * CAP) % LANES, axis=1)
                acc = jnp.where((lane >= j * CAP) & (lane < (j + 1) * CAP), v, acc)
            row.append(acc)
        series.append(jnp.concatenate(row, axis=1))
    x = jnp.concatenate(series, axis=0)
    hi = x.astype(jnp.bfloat16)
    rest = x - hi.astype(jnp.float32)
    mid = rest.astype(jnp.bfloat16)
    lo = (rest - mid.astype(jnp.float32)).astype(jnp.bfloat16)
    r = nt(jnp.concatenate([hi, mid, lo], axis=0), gp_ref[...])
    n = members * STEPS
    r = r[0:n] + r[n : 2 * n] + r[2 * n : 3 * n]
    row8 = iota((SUB, LANES), 0)
    per = LANES // coast
    for m in range(members):
        total = jnp.zeros((SUB, LANES), jnp.float32)
        for l in range(STEPS):
            v = r[m * SUB : (m + 1) * SUB, (l // per) * LANES : (l // per + 1) * LANES]
            if l % per:
                v = pltpu.roll(v, LANES - (l % per) * coast, axis=1)
            if l:
                v = jnp.where(row8 >= l, pltpu.roll(v, l, axis=0), 0.0)
            total = total + v
        out_ref[m * SUB : (m + 1) * SUB, :] = (prior_ref[m * SUB : (m + 1) * SUB, :] + few_ref[m * SUB : (m + 1) * SUB, :]) + total[:, 0:coast]


def local(eta_init, depth, sea_mask, probe_cells, elapsed_record, gauge_kernels):
    members, lat_cells, lon_cells = eta_init.shape
    lat_count = lax.axis_size("lat")
    lon_count = lax.axis_size("lon")
    coast, probes, lag_count = gauge_kernels.shape[1:]
    total_lat = lat_cells * lat_count
    total_lon = lon_cells * lon_count
    spacing = 2.0 * math.pi / total_lon
    courant = courant_for(total_lat, spacing)
    tiles = lon_cells // LANES
    total = lat_cells + 2 * HALO
    stride = total * tiles + total + SUB
    slots = lon_count * CAP
    f32 = jnp.float32
    vmem = pl.BlockSpec(memory_space=pltpu.VMEM)
    smem = pl.BlockSpec(memory_space=pltpu.SMEM)
    hbm = pl.BlockSpec(memory_space=pltpu.HBM)
    dma = pltpu.SemaphoreType.DMA

    def limit(mib):
        return pltpu.CompilerParams(vmem_limit_bytes=mib * MIB)

    def cost(us):
        return pl.CostEstimate(flops=0, bytes_accessed=int(us * 3.0e6), transcendentals=0)

    def stay(*arrays):
        return [pltpu.with_memory_space_constraint(a, pltpu.HBM) for a in arrays]

    halo_shape = jax.ShapeDtypeStruct(((members + 1) * HALO * tiles, LANES), f32)
    first_rows, last_rows = pl.pallas_call(
        functools.partial(rows_kernel, members),
        out_shape=[halo_shape] * 2,
        in_specs=[hbm] * 3,
        out_specs=[vmem] * 2,
        scratch_shapes=[
            pltpu.VMEM((2, members, HALO, lon_cells), f32),
            pltpu.VMEM((2, HALO, lon_cells), f32),
            pltpu.VMEM((2, HALO, lon_cells), jnp.int32),
            dma((2, 3)),
        ],
        compiler_params=limit(8),
        cost_estimate=cost(1),
        name="rows",
    )(*stay(eta_init, depth, sea_mask))
    up = [(i, i + 1) for i in range(lat_count - 1)]
    down = [(i + 1, i) for i in range(lat_count - 1)]
    top = lax.ppermute(last_rows, "lat", up)
    bottom = lax.ppermute(first_rows, "lat", down)

    first_row = lax.axis_index("lat") * lat_cells - HALO
    ids = (first_row + jnp.arange(total, dtype=jnp.int32)).astype(f32)
    latitude = -0.5 * total_lat * spacing + (ids + 0.5) * spacing
    scale = courant / jnp.cos(latitude)
    factors = jnp.stack([scale * scale, courant * jnp.cos(latitude + 0.5 * spacing), scale])
    factors = jnp.broadcast_to(factors[:, :, None], (3, total, LANES)).reshape(3 * total, LANES)

    strip = jax.ShapeDtypeStruct((DEEP * SUB, LANES), f32)
    sent, one, two, own, pick = pl.pallas_call(
        functools.partial(table_kernel, lat_cells, lon_cells, lat_count, lon_count, members),
        out_shape=[
            jax.ShapeDtypeStruct((lon_count, 1, LANES), jnp.int32),
            strip,
            strip,
            jax.ShapeDtypeStruct(((members + 1) * total, LANES), f32),
            jax.ShapeDtypeStruct((slots, probes), jnp.bfloat16),
        ],
        in_specs=[hbm] * 4,
        out_specs=[vmem] * 5,
        scratch_shapes=[
            pltpu.VMEM((2, members, lat_cells, LANES), f32),
            pltpu.VMEM((2, lat_cells, LANES), f32),
            pltpu.VMEM((2, lat_cells, LANES), jnp.int32),
            pltpu.VMEM(probe_cells.shape[1:], jnp.int32),
            dma((2, 3)),
            dma((1,)),
        ],
        compiler_params=limit(8),
        cost_estimate=cost(1.5),
        name="table",
    )(*stay(probe_cells, eta_init, depth, sea_mask))
    incoming = lax.all_to_all(sent, "lon", split_axis=0, concat_axis=0, tiled=True)

    odd = jnp.broadcast_to(lax.rem(lax.axis_index("lon"), 2).astype(jnp.int32), (1, LANES))
    send_a, send_b = pl.pallas_call(
        functools.partial(rim_kernel, members),
        out_shape=[strip] * 2,
        in_specs=[vmem] * 5,
        out_specs=[vmem] * 2,
        compiler_params=limit(8),
        cost_estimate=cost(0.5),
        name="rim",
    )(odd, one, two, top, bottom)
    swap_a = [(i, i ^ 1) for i in range(lon_count)]
    swap_b = [((i + 1) % lon_count, ((i ^ 1) + 1) % lon_count) for i in range(lon_count)]
    rim_a = lax.ppermute(send_a, "lon", swap_a)
    rim_b = lax.ppermute(send_b, "lon", swap_b)

    few = 2 * KTILE
    half = (probes - few) // 2

    def past_sum(size, first, count, after, name, us):
        return pl.pallas_call(
            functools.partial(past_kernel, members),
            grid=(count,),
            out_shape=jax.ShapeDtypeStruct((members * STEPS, coast), f32),
            in_specs=[
                pl.BlockSpec((None, coast, size, lag_count), lambda k: (0, 0, k + first, 0)),
                pl.BlockSpec((None, members, size, lag_count), lambda k: (0, 0, k + first, 0)),
                pl.BlockSpec((SUB, LANES), lambda k: (0, 0)),
            ],
            out_specs=pl.BlockSpec((members * STEPS, coast), lambda k: (0, 0)),
            scratch_shapes=[pltpu.VMEM((coast * KTILE, members * STEPS * KTILE), f32)],
            compiler_params=limit(26),
            cost_estimate=cost(us),
            name=name,
        )(*stay(gauge_kernels, elapsed_record), after)

    prior_few = past_sum(few, (probes - few) // few, 1, send_a, "past_few", 1.5)

    field = pltpu.VMEM((total * tiles, LANES), f32)
    tall = pltpu.VMEM((total + SUB, LANES), f32)
    eta_final, samples, recent = pl.pallas_call(
        functools.partial(wave_kernel, members, stride),
        out_shape=[
            jax.ShapeDtypeStruct(eta_init.shape, f32),
            jax.ShapeDtypeStruct((lon_count, SUB, LANES), f32),
            jax.ShapeDtypeStruct((STEPS * coast, slots), jnp.bfloat16),
        ],
        in_specs=[vmem] * 4 + [hbm] * 4 + [vmem] * 6,
        out_specs=[hbm, vmem, vmem],
        scratch_shapes=[
            pltpu.VMEM(eta_init.shape, f32),
            pltpu.VMEM(depth.shape, f32),
            pltpu.VMEM(depth.shape, jnp.int32),
            field,
            field,
            field,
            field,
            tall,
            tall,
            tall,
            pltpu.VMEM(eta_init.shape, f32),
            pltpu.SMEM((lon_count, 1, LANES), jnp.int32),
            pltpu.VMEM((coast, probes, LANES), jnp.bfloat16),
            pltpu.VMEM((coast * SUB, probes), f32),
            dma((PARTS, 3)),
            dma((PARTS,)),
            dma((2,)),
        ]
        + [pltpu.VMEM(((STEPS + 1) * stride, LANES), f32)] * members
        + [field] * members
        + [tall] * (2 * members),
        compiler_params=limit(36),
        cost_estimate=cost(11),
        name="wave",
    )(odd, incoming, prior_few, pick, *stay(eta_init, depth, sea_mask, gauge_kernels), top, bottom, rim_a, rim_b, own, factors)

    answered = lax.all_to_all(samples, "lon", split_axis=0, concat_axis=0, tiled=True)
    prior = past_sum(half, 0, 2, samples.reshape(-1, LANES), "past", 6)
    shore = pl.pallas_call(
        functools.partial(shore_kernel, members),
        out_shape=jax.ShapeDtypeStruct((members * STEPS, coast), f32),
        in_specs=[vmem] * 4,
        out_specs=vmem,
        compiler_params=limit(8),
        cost_estimate=cost(1),
        name="shore",
    )(answered, recent, prior, prior_few)
    return eta_final, shore.reshape(1, members, STEPS, coast)


def solution(mesh):
    in_specs = (
        P(None, "lat", "lon"),
        P("lat", "lon"),
        P("lat", "lon"),
        P(("lon", "lat"), None, None),
        P(("lon", "lat"), None, None, None),
        P(("lon", "lat"), None, None, None),
    )
    out_specs = (P(None, "lat", "lon"), P(("lon", "lat"), None, None, None))
    return jax.shard_map(local, mesh=mesh, in_specs=in_specs, out_specs=out_specs, check_vma=False)
```
